32 devices in a mesh: groups: 2 (over x), engine: 2 (over core), tp: 8 (over z, y).
Axes of the slice: x: 2, y: 2, z: 4, core: 2. Of those that a mesh axis runs over, the one named last changes fastest.
Arguments:
- tokens: bfloat16 [4096, 8192], P(('groups', 'engine'), 'tp'), parts along dimension 0, may hold values from -200 to 200
- norm_gain: float32 [8192], replicated, may hold values from 0.1 to 1.9
- qkv_weight: bfloat16 [8192, 10240], P(('engine', 'tp')), may hold values from -0.0625 to 0.0625
Outputs:
- projections: bfloat16 [4096, 10240], P(('groups', 'engine'), 'tp'), parts along dimension 0
The draws below stay inside these ranges and needn't reach their ends.
There are 2 independent parts, one for each index of `groups`. The reference program is written for one: setup_inputs(seed, part) draws one part's arguments, and reference() takes and returns one part's arrays. A program takes and returns all parts, laid end to end along the dimension named above; an argument that names none is the same for every part. Nothing has to cross between parts.
All inputs are finite; a program needn't handle non-finite values.
Results may differ from the reference program's by a relative error of at most 0.0049.
Values may be sent and summed in bfloat16 or wider, within the bound.
A program may use at most 192 MiB of HBM per device.

```python
import math
import jax
import jax.numpy as jnp
from jax import lax

D = 8192
QKV = 10240
TOKENS = 2048


def draw_tokens(key, part):
    key = jax.random.fold_in(key, 1)
    streams = jax.random.split(key, 3)
    row_scale = jnp.exp(jax.random.uniform(streams[0], (TOKENS, 1), jnp.float32, 0.0, math.log(10.0)))
    column_scale = jnp.exp(jax.random.uniform(streams[1], (1, D), jnp.float32, math.log(0.5), math.log(5.0)))
    base_values = jnp.clip(jax.random.normal(streams[2], (TOKENS, D), jnp.float32), -4.0, 4.0)
    return (base_values * row_scale * column_scale).astype(jnp.bfloat16)


def block_scale(stream_key, extent, shards, low, top_value):
    loudness, own = 1.0, jax.random.fold_in(stream_key, 6)
    for dim, blocks in shards:
        draws = jnp.exp(jax.random.uniform(jax.random.fold_in(own, dim), (blocks,), jnp.float32, low / len(shards), top_value / len(shards)))
        loudness = loudness * jnp.repeat(draws, extent[dim] // blocks).reshape([-1 if axis == dim else 1 for axis in range(len(extent))])
    return loudness


def bell_draw(own_key, extent, spread, reach, cuts=(), held_as=jnp.bfloat16):
    factor_of = block_scale(own_key, extent, cuts, -0.22, 0.18) if cuts else 1.0
    entries = jax.random.normal(own_key, extent, jnp.float32) * spread * factor_of
    return jnp.minimum(jnp.maximum(entries, -reach), reach).astype(held_as)


def setup_inputs(seed: int = 0, part: int = 0) -> dict:
    seeds = jax.random.split(jax.random.key(seed), 4)
    part_splits = jax.random.split(jax.random.fold_in(seeds[3], part), 4)
    tokens = draw_tokens(jax.random.fold_in(jax.random.fold_in(seeds[3], part), 71), part)
    norm_gain = jnp.clip(1.0 + 0.18 * jax.random.normal(seeds[1], (D,), jnp.float32), 0.1, 1.9)
    qkv_weight = bell_draw(seeds[2], (D, QKV), D ** -0.5, 0.0625, ((0, 16),))
    return dict(tokens=tokens, norm_gain=norm_gain, qkv_weight=qkv_weight)


def reference(tokens, norm_gain, qkv_weight):
    widened = tokens.astype(jnp.float32)
    mean_square = lax.optimization_barrier(jnp.mean(widened * widened, axis=1, keepdims=True))
    normed = (widened * lax.rsqrt(mean_square + 1e-05) * norm_gain[None, :]).astype(jnp.bfloat16)
    return jnp.dot(normed, qkv_weight, preferred_element_type=jnp.float32).astype(jnp.bfloat16)
```

```python
import functools

import jax
import jax.numpy as jnp
from jax import lax
from jax.experimental import pallas as pl
from jax.experimental.pallas import tpu as pltpu
from jax.sharding import PartitionSpec as P

MESH = pl.DeviceIdType.MESH
CHUNKS = 4
EPS = 1e-05


def plain_body(tokens, norm_gain, qkv_weight):
    whole = lax.all_gather(tokens, "tp", axis=1, tiled=True)
    widened = whole.astype(jnp.float32)
    mean_square = jnp.mean(widened * widened, axis=1, keepdims=True)
    normed = (widened * lax.rsqrt(mean_square + EPS) * norm_gain[None, :]).astype(jnp.bfloat16)
    engines = lax.axis_size("engine")
    tensor_ways = lax.axis_size("tp")
    row_count = qkv_weight.shape[0]
    token_rows = normed.shape[0]
    paired = lax.all_gather(qkv_weight, "engine", axis=0, tiled=True)
    dealt = lax.all_to_all(paired, "tp", split_axis=1, concat_axis=0, tiled=True)
    blocks = dealt.reshape(tensor_ways, engines, row_count, dealt.shape[1])
    features = normed.reshape(token_rows, engines, tensor_ways, row_count)
    projected = jnp.einsum("aetr,terc->ac", features, blocks, preferred_element_type=jnp.float32)
    return projected.astype(jnp.bfloat16)


def kernel(rows, depth, width, tok_ref, gain_ref, w_ref, out_ref,
           raw, tbuf, wbuf, pout, pin, total, obuf, squares, scale,
           load_sem, wload_sem, out_sem, send_sem, tz_sem, ty_sem, wd_sem, wx_sem, wc_sem, p_sem, s_sem):
    x = lax.axis_index("groups")
    e = lax.axis_index("engine")
    me = lax.axis_index("tp")
    y = me % 2
    z = me // 2
    zh = z // 2
    zl = z % 2
    inner = (zh + zl) % 2
    features = raw.shape[1]
    depth_all = 4 * features
    chunk = rows // CHUNKS
    part = depth // 2
    counter = [0]
    sent = []

    def tp_at(yy, zz):
        return 2 * zz + yy

    def remote(src, dst, recv, where):
        copy = pltpu.make_async_remote_copy(
            src_ref=src, dst_ref=dst, send_sem=send_sem.at[counter[0]], recv_sem=recv,
            device_id=where, device_id_type=MESH)
        counter[0] += 1
        return copy

    def send(*args):
        copy = remote(*args)
        copy.start()
        sent.append(copy)

    def landed(dst, recv):
        pltpu.make_async_remote_copy(
            src_ref=dst, dst_ref=dst, send_sem=send_sem.at[0], recv_sem=recv,
            device_id={"tp": me}, device_id_type=MESH).wait_recv()

    def crows(q):
        return pl.ds(q * chunk, chunk)

    loads = [pltpu.make_async_copy(tok_ref.at[crows(q)], raw.at[crows(q)], load_sem.at[q]) for q in range(CHUNKS)]
    for load in loads:
        load.start()
    y_other, z_near, z_far = 1 - y, z + 1 - 2 * zl, (z + 2) % 4
    peers = [(y_other, z), (y, z_near), (y_other, z_near)]

    def columns_of(yy, zz, cs):
        owner = tp_at(yy, (zz + 2) % 4 if cs == 0 else zz)
        return pl.ds(pl.multiple_of(owner * width, width), width)

    def block_rows(ee, yy, zz):
        return pl.multiple_of((ee * 4 + (zz % 2) * 2 + yy) * depth, depth)

    mine = block_rows(e, y, z)
    wloads = [
        pltpu.make_async_copy(w_ref.at[:, columns_of(y, z, cs)], wbuf.at[cs, pl.ds(mine, depth)], wload_sem.at[cs])
        for cs in range(2)
    ]
    for load in wloads:
        load.start()

    barrier = pltpu.get_barrier_semaphore()
    for d in range(1, 8):
        pl.semaphore_signal(barrier, inc=1, device_id={"tp": (me + d) % 8}, device_id_type=MESH)
    pl.semaphore_signal(barrier, inc=1, device_id={"groups": 1 - x}, device_id_type=MESH)
    pl.semaphore_signal(barrier, inc=1, device_id={"engine": 1 - e}, device_id_type=MESH)
    pl.semaphore_wait(barrier, 9)

    def send_weights(cs):
        for d, (yy, zz) in enumerate(peers):
            send(w_ref.at[pl.ds(pl.multiple_of(x * part, part), part), columns_of(yy, zz, cs)],
                 wbuf.at[cs, pl.ds(mine + x * part, part)],
                 wd_sem.at[cs * 3 + d], {"tp": tp_at(yy, zz)})
        send(w_ref.at[:, columns_of(y, z, cs)], wbuf.at[cs, pl.ds(mine, depth)],
             wc_sem.at[cs * 7 + 6], {"engine": 1 - e})

    def pass_direct(cs, d):
        region = wbuf.at[cs, pl.ds(block_rows(e, *peers[d]) + x * part, part)]
        landed(region, wd_sem.at[cs * 3 + d])
        send(region, region, wx_sem.at[cs * 3 + d], {"groups": 1 - x})
        send(region, region, wc_sem.at[cs * 7 + d], {"engine": 1 - e})

    def pass_across(cs, d):
        region = wbuf.at[cs, pl.ds(block_rows(e, *peers[d]) + (1 - x) * part, part)]
        landed(region, wx_sem.at[cs * 3 + d])
        send(region, region, wc_sem.at[cs * 7 + 3 + d], {"engine": 1 - e})

    def weights_here(cs):
        for d in range(3):
            first = block_rows(1 - e, *peers[d])
            landed(wbuf.at[cs, pl.ds(first + x * part, part)], wc_sem.at[cs * 7 + d])
            landed(wbuf.at[cs, pl.ds(first + (1 - x) * part, part)], wc_sem.at[cs * 7 + 3 + d])
        landed(wbuf.at[cs, pl.ds(block_rows(1 - e, y, z), depth)], wc_sem.at[cs * 7 + 6])
        wloads[cs].wait()

    send_weights(0)

    def tcols(index):
        return pl.ds(pl.multiple_of(index * features, features), features)

    def tslot(slot, yy, q):
        return tbuf.at[crows(q), tcols(slot * 2 + yy)]

    home, cross = zh, 1 - zh
    own_index = (1 - inner) * (home * 2 + y) + inner * 4
    gain = gain_ref[:, pl.ds(pl.multiple_of(me * features, features), features)]
    z_sends = [remote(tbuf.at[crows(q), tcols(own_index)], tslot(home, y, q), tz_sem.at[inner * CHUNKS + q],
                      {"tp": tp_at(y, z + 1 - 2 * zh)}) for q in range(CHUNKS)]
    z_passes = [remote(tslot(cross, y, q), tslot(cross, y, q), tz_sem.at[CHUNKS + q],
                       {"tp": tp_at(y, z_near)}) for q in range(CHUNKS)]
    y_home = [remote(tslot(home, y, q), tslot(home, y, q), ty_sem.at[home * CHUNKS + q],
                     {"tp": tp_at(y_other, z)}) for q in range(CHUNKS)]
    y_cross = [remote(tslot(cross, y, q), tslot(cross, y, q), ty_sem.at[cross * CHUNKS + q],
                      {"tp": tp_at(y_other, z)}) for q in range(CHUNKS)]

    for q in range(CHUNKS):
        loads[q].wait()
        tbuf[crows(q), tcols(own_index)] = (raw[crows(q)].astype(jnp.float32) * gain).astype(jnp.bfloat16)
        z_sends[q].start()
        if q < 2:
            @pl.when(inner == 0)
            def _():
                y_home[q].start()

    def pass_tokens(q):
        if q >= 2:
            @pl.when(inner == 0)
            def _():
                y_home[q].start()

        @pl.when(inner == 1)
        def _():
            landed(tslot(home, y, q), tz_sem.at[q])
            y_home[q].start()
        landed(tslot(cross, y, q), tz_sem.at[CHUNKS + q])

        @pl.when(inner == 1)
        def _():
            z_passes[q].start()
        y_cross[q].start()

    pass_tokens(0)
    pass_direct(0, 0)
    pass_direct(0, 1)
    pass_tokens(1)
    pass_direct(0, 2)
    pass_tokens(2)
    pass_tokens(3)
    send_weights(1)

    ones = jnp.ones((8, features), jnp.bfloat16)
    contract_last = (((1,), (1,)), ((), ()))
    for q in range(CHUNKS):
        wide = raw[crows(q)].astype(jnp.float32)
        square = wide * wide
        high = square.astype(jnp.bfloat16)
        low = (square - high.astype(jnp.float32)).astype(jnp.bfloat16)
        squares[me, :, crows(q)] = (
            lax.dot_general(ones, high, contract_last, preferred_element_type=jnp.float32)
            + lax.dot_general(ones, low, contract_last, preferred_element_type=jnp.float32))
    for d in range(1, 8):
        send(squares.at[me], squares.at[me], s_sem.at[d], {"tp": (me + d) % 8})
    for d in range(3):
        pass_across(0, d)
    weights_here(0)

    tile = 256

    def multiply(q, cs, put):
        @pl.loop(0, width // tile)
        def _(n):
            cols = pl.ds(pl.multiple_of(n * tile, tile), tile)
            put(cols, jnp.dot(tbuf[crows(q), pl.ds(0, depth_all)], wbuf[cs, :, cols],
                              preferred_element_type=jnp.float32))

    for q in range(CHUNKS):
        for slot in range(2):
            landed(tslot(slot, y_other, q), ty_sem.at[slot * CHUNKS + q])

        def put(cols, value):
            pout[crows(q), cols] = value.astype(jnp.bfloat16)
        multiply(q, 0, put)
        send(pout.at[crows(q)], pin.at[crows(q)], p_sem.at[q], {"tp": tp_at(y, z_far)})
        if q == 1:
            for d in range(3):
                pass_direct(1, d)
    for d in range(3):
        pass_across(1, d)
    for d in range(1, 8):
        landed(squares.at[(me + 8 - d) % 8], s_sem.at[d])
    summed = squares[0]
    for d in range(1, 8):
        summed = summed + squares[d]
    inverse = lax.rsqrt(summed / (8 * features) + EPS)
    scale[...] = jnp.broadcast_to(inverse[0:1], (128, rows)).T
    weights_here(1)
    for q in range(CHUNKS):
        def put(cols, value):
            total[crows(q), cols] = value
        multiply(q, 1, put)
    outs = []
    for q in range(CHUNKS):
        landed(pin.at[crows(q)], p_sem.at[q])
        obuf[crows(q)] = ((total[crows(q)] + pin[crows(q)].astype(jnp.float32)) * scale[crows(q), 0:1]).astype(jnp.bfloat16)
        copy = pltpu.make_async_copy(obuf.at[crows(q)], out_ref.at[crows(q)], out_sem.at[q])
        copy.start()
        outs.append(copy)
    for copy in outs:
        copy.wait()
    for copy in sent + z_sends + y_home + y_cross:
        copy.wait_send()

    @pl.when(inner == 1)
    def _():
        for copy in z_passes:
            copy.wait_send()


def body(tokens, norm_gain, qkv_weight):
    rows, features = tokens.shape
    depth, columns = qkv_weight.shape
    width = columns // 8
    dma = pltpu.SemaphoreType.DMA
    return pl.pallas_call(
        functools.partial(kernel, rows, depth, width),
        out_shape=jax.ShapeDtypeStruct((rows, width), jnp.bfloat16),
        in_specs=[
            pl.BlockSpec(memory_space=pl.ANY),
            pl.BlockSpec(memory_space=pltpu.VMEM),
            pl.BlockSpec(memory_space=pl.ANY),
        ],
        out_specs=pl.BlockSpec(memory_space=pl.ANY),
        scratch_shapes=[
            pltpu.VMEM((rows, features), jnp.bfloat16),
            pltpu.VMEM((rows, 5 * features), jnp.bfloat16),
            pltpu.VMEM((2, 8 * depth, width), jnp.bfloat16),
            pltpu.VMEM((rows, width), jnp.bfloat16),
            pltpu.VMEM((rows, width), jnp.bfloat16),
            pltpu.VMEM((rows, width), jnp.float32),
            pltpu.VMEM((rows, width), jnp.bfloat16),
            pltpu.VMEM((8, 8, rows), jnp.float32),
            pltpu.VMEM((rows, 128), jnp.float32),
            dma((CHUNKS,)), dma((2,)), dma((CHUNKS,)), dma((64,)),
            dma((2 * CHUNKS,)), dma((2 * CHUNKS,)), dma((6,)), dma((6,)), dma((14,)), dma((CHUNKS,)), dma((8,)),
        ],
        compiler_params=pltpu.CompilerParams(
            collective_id=0, has_side_effects=True, vmem_limit_bytes=58 * 1024 * 1024),
        cost_estimate=pl.CostEstimate(
            flops=2 * rows * features * 8 * width, bytes_accessed=20 * 2**20, transcendentals=0),
    )(tokens, norm_gain.reshape(1, -1), qkv_weight)


def solution(mesh):
    placed = (P(("groups", "engine"), "tp"), P(), P(("engine", "tp"), None))
    shape = mesh.shape
    fits = shape["groups"] == 2 and shape["engine"] == 2 and shape["tp"] == 8
    return jax.shard_map(
        body if fits else plain_body, mesh=mesh, in_specs=placed,
        out_specs=P(("groups", "engine"), "tp"), check_vma=False)
```

```python
import functools

import jax
import jax.numpy as jnp
from jax import lax
from jax.experimental import pallas as pl
from jax.experimental.pallas import tpu as pltpu
from jax.sharding import PartitionSpec as P

MESH = pl.DeviceIdType.MESH
CHUNKS = 4
PIECES = 8
AHEAD = 8
SPLIT = 2
DIRECT_AT = 2
ORDER = ("t0", "t1", "d0", "d1", "t2", "t3", "d2", "t4", "t5", "t6", "t7", "w1", "x0", "x1", "x2")
EPS = 1e-05


def plain_body(tokens, norm_gain, qkv_weight):
    whole = lax.all_gather(tokens, "tp", axis=1, tiled=True)
    widened = whole.astype(jnp.float32)
    mean_square = jnp.mean(widened * widened, axis=1, keepdims=True)
    normed = (widened * lax.rsqrt(mean_square + EPS) * norm_gain[None, :]).astype(jnp.bfloat16)
    engines = lax.axis_size("engine")
    tensor_ways = lax.axis_size("tp")
    row_count = qkv_weight.shape[0]
    token_rows = normed.shape[0]
    paired = lax.all_gather(qkv_weight, "engine", axis=0, tiled=True)
    dealt = lax.all_to_all(paired, "tp", split_axis=1, concat_axis=0, tiled=True)
    blocks = dealt.reshape(tensor_ways, engines, row_count, dealt.shape[1])
    features = normed.reshape(token_rows, engines, tensor_ways, row_count)
    projected = jnp.einsum("aetr,terc->ac", features, blocks, preferred_element_type=jnp.float32)
    return projected.astype(jnp.bfloat16)


def kernel(rows, depth, width, tok_ref, gain_ref, w_ref, out_ref,
           raw, tbuf, wbuf, pout, pin, total, obuf, squares, scale,
           load_sem, wload_sem, out_sem, send_sem, tz_sem, ty_sem, wd_sem, wx_sem, wc_sem, p_sem, s_sem):
    x = lax.axis_index("groups")
    e = lax.axis_index("engine")
    me = lax.axis_index("tp")
    y = me % 2
    z = me // 2
    zh = z // 2
    zl = z % 2
    inner = (zh + zl) % 2
    features = raw.shape[1]
    depth_all = 4 * features
    chunk = rows // CHUNKS
    part = depth // 2
    counter = [0]
    sent = []

    def tp_at(yy, zz):
        return 2 * zz + yy

    def remote(src, dst, recv, where):
        copy = pltpu.make_async_remote_copy(
            src_ref=src, dst_ref=dst, send_sem=send_sem.at[counter[0]], recv_sem=recv,
            device_id=where, device_id_type=MESH)
        counter[0] += 1
        return copy

    def send(*args):
        copy = remote(*args)
        copy.start()
        sent.append(copy)

    def landed(dst, recv):
        pltpu.make_async_remote_copy(
            src_ref=dst, dst_ref=dst, send_sem=send_sem.at[0], recv_sem=recv,
            device_id={"tp": me}, device_id_type=MESH).wait_recv()

    def crows(q):
        return pl.ds(q * chunk, chunk)

    def trows(q):
        return pl.ds(q * (rows // PIECES), rows // PIECES)

    loads = [pltpu.make_async_copy(tok_ref.at[trows(q)], raw.at[trows(q)], load_sem.at[q]) for q in range(PIECES)]
    for load in loads:
        load.start()
    y_other, z_near, z_far = 1 - y, z + 1 - 2 * zl, (z + 2) % 4
    peers = [(y_other, z), (y, z_near), (y_other, z_near)]

    span = width // SPLIT

    def columns_of(yy, zz, cs, first=0, count=width):
        owner = tp_at(yy, (zz + 2) % 4 if cs == 0 else zz)
        return pl.ds(pl.multiple_of(owner * width + first, 128), count)

    def block_rows(ee, yy, zz):
        return pl.multiple_of((ee * 4 + (zz % 2) * 2 + yy) * depth, depth)

    mine = block_rows(e, y, z)
    wloads = [
        pltpu.make_async_copy(w_ref.at[:, columns_of(y, z, cs)], wbuf.at[cs, pl.ds(mine, depth)], wload_sem.at[cs])
        for cs in range(2)
    ]
    for load in wloads:
        load.start()

    barrier = pltpu.get_barrier_semaphore()
    for d in range(1, 8):
        pl.semaphore_signal(barrier, inc=1, device_id={"tp": (me + d) % 8}, device_id_type=MESH)
    pl.semaphore_signal(barrier, inc=1, device_id={"groups": 1 - x}, device_id_type=MESH)
    pl.semaphore_signal(barrier, inc=1, device_id={"engine": 1 - e}, device_id_type=MESH)
    pl.semaphore_wait(barrier, 9)

    def piece(cs, ee, d, half):
        h, d = divmod(d, 3)
        return wbuf.at[cs, pl.ds(block_rows(ee, *peers[d]) + half * part, part), pl.ds(h * span, span)]

    def send_weights(cs):
        for d in range(3 * SPLIT):
            h, (yy, zz) = d // 3, peers[d % 3]
            send(w_ref.at[pl.ds(pl.multiple_of(x * part, part), part), columns_of(yy, zz, cs, h * span, span)],
                 wbuf.at[cs, pl.ds(mine + x * part, part), pl.ds(h * span, span)],
                 wd_sem.at[cs * 3 * SPLIT + d], {"tp": tp_at(yy, zz)})
        send(w_ref.at[:, columns_of(y, z, cs)], wbuf.at[cs, pl.ds(mine, depth)],
             wc_sem.at[12 * SPLIT + cs], {"engine": 1 - e})

    def pass_direct(cs, d):
        region = piece(cs, e, d, x)
        landed(region, wd_sem.at[cs * 3 * SPLIT + d])
        send(region, region, wx_sem.at[cs * 3 * SPLIT + d], {"groups": 1 - x})
        send(region, region, wc_sem.at[cs * 6 * SPLIT + d], {"engine": 1 - e})

    def pass_across(cs, d):
        region = piece(cs, e, d, 1 - x)
        landed(region, wx_sem.at[cs * 3 * SPLIT + d])
        send(region, region, wc_sem.at[(cs * 2 + 1) * 3 * SPLIT + d], {"engine": 1 - e})

    def weights_here(cs):
        for d in range(3 * SPLIT):
            landed(piece(cs, 1 - e, d, x), wc_sem.at[cs * 6 * SPLIT + d])
            landed(piece(cs, 1 - e, d, 1 - x), wc_sem.at[(cs * 2 + 1) * 3 * SPLIT + d])
        landed(wbuf.at[cs, pl.ds(block_rows(1 - e, y, z), depth)], wc_sem.at[12 * SPLIT + cs])
        wloads[cs].wait()

    send_weights(0)

    def tcols(index):
        return pl.ds(pl.multiple_of(index * features, features), features)

    def tslot(slot, yy, q):
        return tbuf.at[trows(q), tcols(slot * 2 + yy)]

    home, cross = zh, 1 - zh
    own_index = (1 - inner) * (home * 2 + y) + inner * 4
    gain = gain_ref[:, pl.ds(pl.multiple_of(me * features, features), features)]
    z_sends = [remote(tbuf.at[trows(q), tcols(own_index)], tslot(home, y, q), tz_sem.at[inner * PIECES + q],
                      {"tp": tp_at(y, z + 1 - 2 * zh)}) for q in range(PIECES)]
    z_passes = [remote(tslot(cross, y, q), tslot(cross, y, q), tz_sem.at[PIECES + q],
                       {"tp": tp_at(y, z_near)}) for q in range(PIECES)]
    y_home = [remote(tslot(home, y, q), tslot(home, y, q), ty_sem.at[home * PIECES + q],
                     {"tp": tp_at(y_other, z)}) for q in range(PIECES)]
    y_cross = [remote(tslot(cross, y, q), tslot(cross, y, q), ty_sem.at[cross * PIECES + q],
                      {"tp": tp_at(y_other, z)}) for q in range(PIECES)]

    def send_tokens(q):
        z_sends[q].start()

        @pl.when(inner == 0)
        def _():
            y_home[q].start()

    for q in range(PIECES):
        loads[q].wait()
        tbuf[trows(q), tcols(own_index)] = (raw[trows(q)].astype(jnp.float32) * gain).astype(jnp.bfloat16)
        if q < AHEAD:
            send_tokens(q)

    def pass_tokens(q):
        @pl.when(inner == 1)
        def _():
            landed(tslot(home, y, q), tz_sem.at[q])
            y_home[q].start()
        landed(tslot(cross, y, q), tz_sem.at[PIECES + q])

        @pl.when(inner == 1)
        def _():
            z_passes[q].start()
        y_cross[q].start()
        if q + AHEAD < PIECES:
            send_tokens(q + AHEAD)

    for step in ORDER:
        kind, index = step[0], int(step[1])
        if kind == "t":
            pass_tokens(index)
        elif kind == "w":
            send_weights(index)
        else:
            for h in range(SPLIT):
                (pass_direct if kind == "d" else pass_across)(0, h * 3 + index)

    ones = jnp.ones((8, features), jnp.bfloat16)
    contract_last = (((1,), (1,)), ((), ()))
    for q in range(CHUNKS):
        wide = raw[crows(q)].astype(jnp.float32)
        square = wide * wide
        high = square.astype(jnp.bfloat16)
        low = (square - high.astype(jnp.float32)).astype(jnp.bfloat16)
        squares[me, :, crows(q)] = (
            lax.dot_general(ones, high, contract_last, preferred_element_type=jnp.float32)
            + lax.dot_general(ones, low, contract_last, preferred_element_type=jnp.float32))
    for d in range(1, 8):
        send(squares.at[me], squares.at[me], s_sem.at[d], {"tp": (me + d) % 8})
    weights_here(0)

    tile = 256

    def multiply(q, cs, put):
        @pl.loop(0, width // tile)
        def _(n):
            cols = pl.ds(pl.multiple_of(n * tile, tile), tile)
            put(cols, jnp.dot(tbuf[crows(q), pl.ds(0, depth_all)], wbuf[cs, :, cols],
                              preferred_element_type=jnp.float32))

    for q in range(CHUNKS):
        for slot in range(2):
            for t in range(q * PIECES // CHUNKS, (q + 1) * PIECES // CHUNKS):
                landed(tslot(slot, y_other, t), ty_sem.at[slot * PIECES + t])

        def put(cols, value):
            pout[crows(q), cols] = value.astype(jnp.bfloat16)
        multiply(q, 0, put)
        send(pout.at[crows(q)], pin.at[crows(q)], p_sem.at[q], {"tp": tp_at(y, z_far)})
        if q == DIRECT_AT:
            for d in range(3 * SPLIT):
                pass_direct(1, d)
    for d in range(3 * SPLIT):
        pass_across(1, d)
    for d in range(1, 8):
        landed(squares.at[(me + 8 - d) % 8], s_sem.at[d])
    summed = squares[0]
    for d in range(1, 8):
        summed = summed + squares[d]
    inverse = lax.rsqrt(summed / (8 * features) + EPS)
    scale[...] = jnp.broadcast_to(inverse[0:1], (128, rows)).T
    weights_here(1)
    for q in range(CHUNKS):
        def put(cols, value):
            total[crows(q), cols] = value
        multiply(q, 1, put)
    outs = []
    for q in range(CHUNKS):
        landed(pin.at[crows(q)], p_sem.at[q])
        obuf[crows(q)] = ((total[crows(q)] + pin[crows(q)].astype(jnp.float32)) * scale[crows(q), 0:1]).astype(jnp.bfloat16)
        copy = pltpu.make_async_copy(obuf.at[crows(q)], out_ref.at[crows(q)], out_sem.at[q])
        copy.start()
        outs.append(copy)
    for copy in outs:
        copy.wait()
    for copy in sent + z_sends + y_home + y_cross:
        copy.wait_send()

    @pl.when(inner == 1)
    def _():
        for copy in z_passes:
            copy.wait_send()


def body(tokens, norm_gain, qkv_weight):
    rows, features = tokens.shape
    depth, columns = qkv_weight.shape
    width = columns // 8
    dma = pltpu.SemaphoreType.DMA
    return pl.pallas_call(
        functools.partial(kernel, rows, depth, width),
        out_shape=jax.ShapeDtypeStruct((rows, width), jnp.bfloat16),
        in_specs=[
            pl.BlockSpec(memory_space=pl.ANY),
            pl.BlockSpec(memory_space=pltpu.VMEM),
            pl.BlockSpec(memory_space=pl.ANY),
        ],
        out_specs=pl.BlockSpec(memory_space=pl.ANY),
        scratch_shapes=[
            pltpu.VMEM((rows, features), jnp.bfloat16),
            pltpu.VMEM((rows, 5 * features), jnp.bfloat16),
            pltpu.VMEM((2, 8 * depth, width), jnp.bfloat16),
            pltpu.VMEM((rows, width), jnp.bfloat16),
            pltpu.VMEM((rows, width), jnp.bfloat16),
            pltpu.VMEM((rows, width), jnp.float32),
            pltpu.VMEM((rows, width), jnp.bfloat16),
            pltpu.VMEM((8, 8, rows), jnp.float32),
            pltpu.VMEM((rows, 128), jnp.float32),
            dma((PIECES,)), dma((2,)), dma((CHUNKS,)), dma((4 * PIECES + 24 * SPLIT + 13,)),
            dma((2 * PIECES,)), dma((2 * PIECES,)), dma((6 * SPLIT,)), dma((6 * SPLIT,)), dma((12 * SPLIT + 2,)), dma((CHUNKS,)), dma((8,)),
        ],
        compiler_params=pltpu.CompilerParams(
            collective_id=0, has_side_effects=True, vmem_limit_bytes=58 * 1024 * 1024),
        cost_estimate=pl.CostEstimate(
            flops=2 * rows * features * 8 * width, bytes_accessed=20 * 2**20, transcendentals=0),
    )(tokens, norm_gain.reshape(1, -1), qkv_weight)


def solution(mesh):
    placed = (P(("groups", "engine"), "tp"), P(), P(("engine", "tp"), None))
    shape = mesh.shape
    fits = shape["groups"] == 2 and shape["engine"] == 2 and shape["tp"] == 8
    return jax.shard_map(
        body if fits else plain_body, mesh=mesh, in_specs=placed,
        out_specs=P(("groups", "engine"), "tp"), check_vma=False)
```
